32 devices in a mesh: sample: 8 (over y, x, core), protein: 4 (over z).
Axes of the slice: x: 2, y: 2, z: 4, core: 2. Of those that a mesh axis runs over, the one named last changes fastest.
Arguments:
- proteins: bfloat16 [4096, 2048], P('sample'), may hold values from -34 to 34
- dosage: bfloat16 [4096, 512], P('sample'), may hold values from 0 to 2, as said below
Outputs:
- scores: float32 [512, 2048], P('sample', 'protein')
The draws below stay inside these ranges and needn't reach their ends.
Inputs may be any that keep to these rules, and one draw needn't show every extreme that they name: `dosage`: allele dosages, whole numbers.
All inputs are finite; a program needn't handle non-finite values.
Results may differ from the reference program's by a relative error of at most 0.0003.
Values sent between devices are 32-bit elements; how exact they have to be, the bound alone decides.
A program may use at most 128 MiB of HBM per device.

```python
import math
import jax
import jax.numpy as jnp
from jax import lax

PROTEINS = 2048
SAMPLES = 4096
VARIANTS = 512


def draw_proteins(key, part):
    subkeys = jax.random.split(key, 3)
    independent = jnp.clip(jax.random.normal(subkeys[0], (SAMPLES, PROTEINS), jnp.float32), -6.0, 6.0)
    loadings = jnp.clip(0.3 * jax.random.normal(subkeys[2], (4, PROTEINS), jnp.float32), -1.2, 1.2)
    factors = jnp.clip(jax.random.normal(subkeys[1], (SAMPLES, 4), jnp.float32), -4.0, 4.0)
    summed = independent + factors[:, 0:1] * loadings[0:1, :]
    summed = summed + factors[:, 1:2] * loadings[1:2, :]
    summed = summed + factors[:, 2:3] * loadings[2:3, :]
    summed = summed + factors[:, 3:4] * loadings[3:4, :]
    return summed.astype(jnp.bfloat16)


def draw_dosage(key, part):
    subkeys = jax.random.split(key, 3)
    frequency = jax.random.randint(subkeys[0], (1, VARIANTS), 1, 16)
    stratum = 2 + jnp.arange(SAMPLES, dtype=jnp.int32)[:, None] * 8 // SAMPLES
    threshold = frequency * stratum
    first_allele = jax.random.randint(subkeys[1], (SAMPLES, VARIANTS), 0, 320) < threshold
    second_allele = jax.random.randint(subkeys[2], (SAMPLES, VARIANTS), 0, 320) < threshold
    counted = first_allele.astype(jnp.int32) + second_allele.astype(jnp.int32)
    return counted.astype(jnp.float32).astype(jnp.bfloat16)


def setup_inputs(seed: int = 0) -> dict:
    seeds = jax.random.split(jax.random.key(seed), 3)
    return {
        "proteins": draw_proteins(jax.random.fold_in(seeds[2], 71), 0),
        "dosage": draw_dosage(jax.random.fold_in(seeds[2], 71), 0),
    }


def right_solve(factor, rows):
    return jax.scipy.linalg.solve_triangular(factor, rows.T, lower=True).T

def reference(proteins, dosage):
    sample_count = proteins.shape[0]
    gram = jnp.dot(proteins.T.astype(jnp.float32), proteins.astype(jnp.float32), preferred_element_type=jnp.float32) / sample_count
    cross = jnp.dot(dosage.T.astype(jnp.float32), proteins.astype(jnp.float32), preferred_element_type=jnp.float32)
    protein_sums = lax.optimization_barrier(jnp.sum(proteins, axis=0, dtype=jnp.float32))
    dose_sums = lax.optimization_barrier(jnp.sum(dosage, axis=0, dtype=jnp.float32))
    dose_squares = lax.optimization_barrier(jnp.sum(dosage * dosage, axis=0, dtype=jnp.float32))
    means = dose_sums / sample_count
    spread = jnp.sqrt(dose_squares / sample_count - means * means + 1e-05)
    centred = (cross - means[:, None] * protein_sums[None, :]) / (spread[:, None] * math.sqrt(sample_count))
    factor = jnp.linalg.cholesky(gram)
    return right_solve(factor, centred)
```

```python
import math

import jax
import jax.numpy as jnp
from jax import lax
from jax.experimental import pallas as pl
from jax.experimental.pallas import tpu as pltpu
from jax.sharding import PartitionSpec as P

SUB = 8
HALF = 128
WIDE = 256
CHUNK = 512


def split(value):
    high = value.astype(jnp.bfloat16)
    low = (value - high.astype(jnp.float32)).astype(jnp.bfloat16)
    return high, low


def dot_nt(left, right):
    return lax.dot_general(
        left, right, (((1,), (1,)), ((), ())), preferred_element_type=jnp.float32
    )


def product_nt(left, right):
    left_high, left_low = left
    right_high, right_low = right
    return (
        dot_nt(left_high, right_high)
        + dot_nt(left_low, right_high)
        + dot_nt(left_high, right_low)
    )


def exact_dot(left, right):
    return jnp.dot(
        left, right, precision=lax.Precision.HIGHEST, preferred_element_type=jnp.float32
    )


def exact_nt(left, right):
    return lax.dot_general(
        left,
        right,
        (((1,), (1,)), ((), ())),
        precision=lax.Precision.HIGHEST,
        preferred_element_type=jnp.float32,
    )


def inverse_factor(work, inverse):
    for start in range(0, HALF, SUB):
        stop = start + SUB
        rows = work[start:stop, :]
        row = [jnp.broadcast_to(rows[k : k + 1, :], (SUB, 2 * HALF)) for k in range(SUB)]
        col = [
            jnp.broadcast_to(rows[:, start + k : start + k + 1], (SUB, HALF)) for k in range(SUB)
        ]
        entry = [
            [jnp.broadcast_to(col[k][i : i + 1, :], (SUB, HALF)) for k in range(i + 1)]
            for i in range(SUB)
        ]
        scale = [None] * SUB
        lower = [[None] * SUB for _ in range(SUB)]
        for k in range(SUB):
            scale[k] = lax.rsqrt(entry[k][k])
            for i in range(k + 1, SUB):
                lower[i][k] = entry[i][k] * scale[k]
            for i in range(k + 1, SUB):
                for m in range(k + 1, i + 1):
                    entry[i][m] = entry[i][m] - lower[i][k] * lower[m][k]
        solved = [None] * SUB
        wide = lambda value: jnp.concatenate([value, value], 1)
        for i in range(SUB):
            total = row[i]
            for k in range(i):
                total = total - wide(lower[i][k]) * solved[k]
            solved[i] = total * wide(scale[i])
        for i in range(SUB):
            inverse[start + i : start + i + 1, :] = solved[i][0:1, HALF:]
        if stop == HALF:
            break
        twice = [None] * SUB
        for i in reversed(range(SUB)):
            total = solved[i]
            for k in range(i + 1, SUB):
                total = total - wide(lower[k][i]) * twice[k]
            twice[i] = total * wide(scale[i])
        for top in range(stop, HALF, SUB):
            block = work[top : top + SUB, :]
            for k in range(SUB):
                factor = jnp.broadcast_to(
                    work[top : top + SUB, start + k : start + k + 1], (SUB, HALF)
                )
                block = block - wide(factor) * twice[k]
            work[top : top + SUB, :] = block


def factor_kernel(gram, centred, out, matrix, work, first, second, full, high, low, sem):
    panels, proteins, _ = gram.shape
    variants = centred.shape[0]
    total = proteins + variants
    copies = [
        pltpu.make_async_copy(gram.at[p], matrix.at[p, pl.ds(0, proteins), :], sem.at[p])
        for p in range(panels)
    ]
    for copy in copies:
        copy.start()
    for p in range(panels):
        matrix[p, proteins:, :] = centred[:, p * WIDE : (p + 1) * WIDE]
    for copy in copies:
        copy.wait()
    eye = (
        lax.broadcasted_iota(jnp.int32, (HALF, HALF), 0)
        == lax.broadcasted_iota(jnp.int32, (HALF, HALF), 1)
    ).astype(jnp.float32)

    def step(k, carry):
        top = pl.multiple_of(k * WIDE, WIDE)
        mid = pl.multiple_of(k * WIDE + HALF, HALF)
        work[:, :HALF] = matrix[k, pl.ds(top, HALF), :HALF]
        work[:, HALF:] = eye
        inverse_factor(work, first)
        below = exact_nt(matrix[k, pl.ds(mid, HALF), :HALF], first[...])
        work[:, :HALF] = matrix[k, pl.ds(mid, HALF), HALF:] - exact_nt(below, below)
        work[:, HALF:] = eye
        inverse_factor(work, second)
        full[:HALF, :HALF] = first[...]
        full[:HALF, HALF:] = jnp.zeros((HALF, HALF), jnp.float32)
        full[HALF:, :HALF] = -exact_dot(second[...], exact_dot(below, first[...]))
        full[HALF:, HALF:] = second[...]
        inverse = split(full[...])

        def panel_chunk(i, carry):
            base = pl.multiple_of(total - CHUNK * (i + 1), 64)
            block = product_nt(split(matrix[k, pl.ds(base, CHUNK), :]), inverse)
            block_high, block_low = split(block)
            high[pl.ds(base, CHUNK), :] = block_high
            low[pl.ds(base, CHUNK), :] = block_low

            @pl.when(i == 0)
            def _():
                out[k] = block[CHUNK - variants :, :]

            return carry

        rest = total - WIDE * (k + 1)
        lax.fori_loop(0, (rest + CHUNK - 1) // CHUNK, panel_chunk, 0)

        def update(m, carry):
            at = pl.multiple_of(m * WIDE, WIDE)
            right = (high[pl.ds(at, WIDE), :], low[pl.ds(at, WIDE), :])

            def update_chunk(i, carry):
                base = pl.multiple_of(total - CHUNK * (i + 1), 64)
                rows = pl.ds(base, CHUNK)
                matrix[m, rows, :] = matrix[m, rows, :] - product_nt(
                    (high[rows, :], low[rows, :]), right
                )
                return carry

            return lax.fori_loop(0, (total - m * WIDE + CHUNK - 1) // CHUNK, update_chunk, carry)

        lax.fori_loop(k + 1, panels, update, 0)
        return carry

    lax.fori_loop(0, panels, step, 0)


def whitened(gram, centred):
    panels, proteins, _ = gram.shape
    variants = centred.shape[0]
    total = proteins + variants
    return pl.pallas_call(
        factor_kernel,
        out_shape=jax.ShapeDtypeStruct((panels, variants, WIDE), jnp.float32),
        in_specs=[
            pl.BlockSpec(memory_space=pl.ANY),
            pl.BlockSpec(memory_space=pltpu.VMEM),
        ],
        out_specs=pl.BlockSpec(memory_space=pltpu.VMEM),
        scratch_shapes=[
            pltpu.VMEM((panels, total, WIDE), jnp.float32),
            pltpu.VMEM((HALF, 2 * HALF), jnp.float32),
            pltpu.VMEM((HALF, HALF), jnp.float32),
            pltpu.VMEM((HALF, HALF), jnp.float32),
            pltpu.VMEM((WIDE, WIDE), jnp.float32),
            pltpu.VMEM((total, WIDE), jnp.bfloat16),
            pltpu.VMEM((total, WIDE), jnp.bfloat16),
            pltpu.SemaphoreType.DMA((panels,)),
        ],
        compiler_params=pltpu.CompilerParams(vmem_limit_bytes=48 * 1024 * 1024),
    )(gram, centred)


def body(proteins, dosage):
    total_proteins = proteins.shape[1]
    groups = lax.axis_size("protein")
    block_width = total_proteins // groups
    column = lax.axis_index("protein")
    sample_count = proteins.shape[0] * lax.axis_size("sample")
    variant_rows = dosage.shape[1] // lax.axis_size("sample")
    contract = (((0,), (0,)), ((), ()))
    own_proteins = lax.dynamic_slice_in_dim(proteins, column * block_width, block_width, 1)
    gram_part = jnp.stack(
        [
            lax.dot_general(
                proteins,
                own_proteins[:, p * WIDE : (p + 1) * WIDE],
                contract,
                preferred_element_type=jnp.float32,
            )
            for p in range(block_width // WIDE)
        ]
    )
    cross_part = lax.dot_general(dosage, own_proteins, contract, preferred_element_type=jnp.float32)
    protein_sums = jnp.sum(own_proteins, axis=0, dtype=jnp.float32)
    dose_sums = jnp.sum(dosage, axis=0, dtype=jnp.float32)
    dose_squares = jnp.sum(dosage * dosage, axis=0, dtype=jnp.float32)
    gram_total, protein_sums, dose_sums, dose_squares = lax.psum(
        (gram_part, protein_sums, dose_sums, dose_squares), "sample"
    )
    cross = lax.psum_scatter(cross_part, "sample", scatter_dimension=0, tiled=True)
    row_start = lax.axis_index("sample") * variant_rows
    dose_sums = lax.dynamic_slice_in_dim(dose_sums, row_start, variant_rows, 0)
    dose_squares = lax.dynamic_slice_in_dim(dose_squares, row_start, variant_rows, 0)
    gram = gram_total / sample_count
    means = dose_sums / sample_count
    spread = jnp.sqrt(dose_squares / sample_count - means * means + 1e-05)
    centred = (cross - means[:, None] * protein_sums[None, :]) / (
        spread[:, None] * math.sqrt(sample_count)
    )
    gram = lax.all_gather(gram, "protein", axis=0, tiled=True)
    centred = lax.all_gather(centred, "protein", axis=1, tiled=True)
    scores = whitened(gram, centred)
    own = block_width // WIDE
    scores = lax.dynamic_slice_in_dim(scores, column * own, own, 0)
    return jnp.concatenate([scores[p] for p in range(own)], 1)


def solution(mesh):
    in_specs = (P("sample", None), P("sample", None))
    out_specs = P("sample", "protein")
    return jax.shard_map(body, mesh=mesh, in_specs=in_specs, out_specs=out_specs, check_vma=False)
```

```python
import math

import jax
import jax.numpy as jnp
from jax import lax
from jax.experimental import pallas as pl
from jax.experimental.pallas import tpu as pltpu
from jax.sharding import PartitionSpec as P

SUB = 8
HALF = 128
WIDE = 256
CHUNK = 512


def split(value):
    high = value.astype(jnp.bfloat16)
    low = (value - high.astype(jnp.float32)).astype(jnp.bfloat16)
    return high, low


def dot_nt(left, right):
    return lax.dot_general(
        left, right, (((1,), (1,)), ((), ())), preferred_element_type=jnp.float32
    )


def product_nt(left, right):
    left_high, left_low = left
    right_high, right_low = right
    return (
        dot_nt(left_high, right_high)
        + dot_nt(left_low, right_high)
        + dot_nt(left_high, right_low)
    )


def exact_dot(left, right):
    return jnp.dot(
        left, right, precision=lax.Precision.HIGHEST, preferred_element_type=jnp.float32
    )


def exact_nt(left, right):
    return lax.dot_general(
        left,
        right,
        (((1,), (1,)), ((), ())),
        precision=lax.Precision.HIGHEST,
        preferred_element_type=jnp.float32,
    )


def inverse_factor(work, inverse):
    for start in range(0, HALF, SUB):
        stop = start + SUB
        rows = work[start:stop, :]
        row = [jnp.broadcast_to(rows[k : k + 1, :], (SUB, 2 * HALF)) for k in range(SUB)]
        col = [
            jnp.broadcast_to(rows[:, start + k : start + k + 1], (SUB, HALF)) for k in range(SUB)
        ]
        entry = [
            [jnp.broadcast_to(col[k][i : i + 1, :], (SUB, HALF)) for k in range(i + 1)]
            for i in range(SUB)
        ]
        scale = [None] * SUB
        lower = [[None] * SUB for _ in range(SUB)]
        for k in range(SUB):
            scale[k] = lax.rsqrt(entry[k][k])
            for i in range(k + 1, SUB):
                lower[i][k] = entry[i][k] * scale[k]
            for i in range(k + 1, SUB):
                for m in range(k + 1, i + 1):
                    entry[i][m] = entry[i][m] - lower[i][k] * lower[m][k]
        solved = [None] * SUB
        wide = lambda value: jnp.concatenate([value, value], 1)
        for i in range(SUB):
            total = row[i]
            for k in range(i):
                total = total - wide(lower[i][k]) * solved[k]
            solved[i] = total * wide(scale[i])
        for i in range(SUB):
            inverse[start + i : start + i + 1, :] = solved[i][0:1, HALF:]
        if stop == HALF:
            break
        twice = [None] * SUB
        for i in reversed(range(SUB)):
            total = solved[i]
            for k in range(i + 1, SUB):
                total = total - wide(lower[k][i]) * twice[k]
            twice[i] = total * wide(scale[i])
        for top in range(stop, HALF, SUB):
            block = work[top : top + SUB, :]
            for k in range(SUB):
                factor = jnp.broadcast_to(
                    work[top : top + SUB, start + k : start + k + 1], (SUB, HALF)
                )
                block = block - wide(factor) * twice[k]
            work[top : top + SUB, :] = block


def factor_kernel(gram, centred, out, matrix, work, first, second, full, high, low, sem):
    groups = gram.shape[0]
    panels = 2 * groups
    proteins = panels * WIDE
    variants = centred.shape[1]
    total = proteins + variants
    copies = []
    for z in range(groups):
        cut = (panels - z) * WIDE
        for p, start, size in ((z, 0, cut), (panels - 1 - z, cut, (z + 1) * WIDE)):
            copies.append(
                pltpu.make_async_copy(
                    gram.at[z, pl.ds(start, size), :],
                    matrix.at[p, pl.ds(p * WIDE, size), :],
                    sem.at[p],
                )
            )
    for copy in copies:
        copy.start()
    for z in range(groups):
        matrix[z, proteins:, :] = centred[z, :, :WIDE]
        matrix[panels - 1 - z, proteins:, :] = centred[z, :, WIDE:]
    for copy in copies:
        copy.wait()
    eye = (
        lax.broadcasted_iota(jnp.int32, (HALF, HALF), 0)
        == lax.broadcasted_iota(jnp.int32, (HALF, HALF), 1)
    ).astype(jnp.float32)

    def step(k, carry):
        top = pl.multiple_of(k * WIDE, WIDE)
        mid = pl.multiple_of(k * WIDE + HALF, HALF)
        work[:, :HALF] = matrix[k, pl.ds(top, HALF), :HALF]
        work[:, HALF:] = eye
        inverse_factor(work, first)
        below = exact_nt(matrix[k, pl.ds(mid, HALF), :HALF], first[...])
        work[:, :HALF] = matrix[k, pl.ds(mid, HALF), HALF:] - exact_nt(below, below)
        work[:, HALF:] = eye
        inverse_factor(work, second)
        full[:HALF, :HALF] = first[...]
        full[:HALF, HALF:] = jnp.zeros((HALF, HALF), jnp.float32)
        full[HALF:, :HALF] = -exact_dot(second[...], exact_dot(below, first[...]))
        full[HALF:, HALF:] = second[...]
        inverse = split(full[...])

        def panel_chunk(i, carry):
            base = pl.multiple_of(total - CHUNK * (i + 1), 64)
            block = product_nt(split(matrix[k, pl.ds(base, CHUNK), :]), inverse)
            block_high, block_low = split(block)
            high[pl.ds(base, CHUNK), :] = block_high
            low[pl.ds(base, CHUNK), :] = block_low

            @pl.when(i == 0)
            def _():
                out[k] = block[CHUNK - variants :, :]

            return carry

        rest = total - WIDE * (k + 1)
        lax.fori_loop(0, (rest + CHUNK - 1) // CHUNK, panel_chunk, 0)

        def update(m, carry):
            at = pl.multiple_of(m * WIDE, WIDE)
            right = (high[pl.ds(at, WIDE), :], low[pl.ds(at, WIDE), :])

            def update_chunk(i, carry):
                base = pl.multiple_of(total - CHUNK * (i + 1), 64)
                rows = pl.ds(base, CHUNK)
                matrix[m, rows, :] = matrix[m, rows, :] - product_nt(
                    (high[rows, :], low[rows, :]), right
                )
                return carry

            return lax.fori_loop(0, (total - m * WIDE + CHUNK - 1) // CHUNK, update_chunk, carry)

        lax.fori_loop(k + 1, panels, update, 0)
        return carry

    lax.fori_loop(0, panels, step, 0)


def whitened(gram, centred):
    panels = 2 * gram.shape[0]
    variants = centred.shape[1]
    total = panels * WIDE + variants
    return pl.pallas_call(
        factor_kernel,
        out_shape=jax.ShapeDtypeStruct((panels, variants, WIDE), jnp.float32),
        in_specs=[
            pl.BlockSpec(memory_space=pl.ANY),
            pl.BlockSpec(memory_space=pltpu.VMEM),
        ],
        out_specs=pl.BlockSpec(memory_space=pltpu.VMEM),
        scratch_shapes=[
            pltpu.VMEM((panels, total, WIDE), jnp.float32),
            pltpu.VMEM((HALF, 2 * HALF), jnp.float32),
            pltpu.VMEM((HALF, HALF), jnp.float32),
            pltpu.VMEM((HALF, HALF), jnp.float32),
            pltpu.VMEM((WIDE, WIDE), jnp.float32),
            pltpu.VMEM((total, WIDE), jnp.bfloat16),
            pltpu.VMEM((total, WIDE), jnp.bfloat16),
            pltpu.SemaphoreType.DMA((panels,)),
        ],
        compiler_params=pltpu.CompilerParams(vmem_limit_bytes=48 * 1024 * 1024),
    )(gram, centred)


def dot_tn(left, right):
    return lax.dot_general(
        left, right, (((0,), (0,)), ((), ())), preferred_element_type=jnp.float32
    )


def gather_kernel(
    chips,
    groups,
    proteins,
    dosage,
    full,
    centred,
    gram_part,
    rest_part,
    gram_pair,
    rest_pair,
    gram_in,
    rest_in,
    piece,
    own_centred,
    pair_send,
    pair_recv,
    chip_send,
    chip_recv,
    z_send,
    z_recv,
    plane_send,
    plane_recv,
    core_send,
    core_recv,
    local_sem,
):
    me = lax.axis_index("sample")
    z = lax.axis_index("protein")
    chip, core = me // 2, me % 2
    partner = (chip * 2 + 1 - core, z)
    samples = proteins.shape[0]
    count = samples * 2 * chips
    variants = dosage.shape[1] // (2 * chips)
    rows = full.shape[1] // (2 * chips)
    panels = 2 * groups
    rest_rows = rest_part.shape[2]

    def chip_at(d):
        return (((chip + d) % chips) * 2 + core, z)

    def z_at(d):
        return (me, (z + d) % groups)

    barrier = pltpu.get_barrier_semaphore()
    peers = [partner]
    peers += [chip_at(d) for d in range(1, chips)]
    peers += [z_at(d) for d in range(1, groups)]
    for peer in peers:
        pl.semaphore_signal(barrier, inc=1, device_id=peer, device_id_type=pl.DeviceIdType.MESH)

    def gram_block(i, carry):
        later = (i + z) // panels
        row = pl.multiple_of((z + i - later * (z + 1)) * WIDE, WIDE)
        column = pl.multiple_of((z + later * (panels - 1 - 2 * z)) * WIDE, WIDE)
        gram_part[pl.ds(pl.multiple_of(i * WIDE, WIDE), WIDE), :] = dot_tn(
            proteins[:, pl.ds(row, WIDE)], proteins[:, pl.ds(column, WIDE)]
        )
        return carry

    lax.fori_loop(0, panels + 1, gram_block, 0)
    first = proteins[:, pl.ds(pl.multiple_of(z * WIDE, WIDE), WIDE)]
    last = proteins[:, pl.ds(pl.multiple_of((panels - 1 - z) * WIDE, WIDE), WIDE)]
    ones = jnp.ones((samples, HALF), jnp.bfloat16)
    doses = dosage[...]
    tables = (
        dot_tn(doses, first),
        dot_tn(doses, last),
        jnp.concatenate([dot_tn(doses, ones), dot_tn(doses * doses, ones)], 1),
    )
    sums = [
        jnp.dot(
            jnp.ones((8, samples), jnp.bfloat16), side, preferred_element_type=jnp.float32
        )
        for side in (first, last)
    ]
    for owner in range(2 * chips):
        for t in range(3):
            rest_part[owner % 2, owner // 2, t * variants : (t + 1) * variants, :] = tables[t][
                owner * variants : (owner + 1) * variants
            ]
        for t in range(2):
            at = 3 * variants + 8 * t
            rest_part[owner % 2, owner // 2, at : at + 8, :] = sums[t]
    pl.semaphore_wait(barrier, len(peers))

    def remote(source, target, send, recv, device):
        copy = pltpu.make_async_remote_copy(
            src_ref=source,
            dst_ref=target,
            send_sem=send,
            recv_sem=recv,
            device_id=device,
            device_id_type=pl.DeviceIdType.MESH,
        )
        copy.start()
        return copy

    def own_rows(owner_core, owner_chip):
        return pl.ds(pl.multiple_of((owner_core * chips + owner_chip) * rows, 8), rows)

    half_rows = chips * rows
    pairs = [
        remote(
            gram_part.at[pl.ds(pl.multiple_of((1 - core) * half_rows, 8), half_rows), :],
            gram_pair,
            pair_send.at[0],
            pair_recv.at[0],
            partner,
        ),
        remote(rest_part.at[1 - core], rest_pair, pair_send.at[1], pair_recv.at[1], partner),
    ]
    for copy in pairs:
        copy.wait()
    sends = []
    for d in list(range(1, chips)) + [0]:
        to = (chip + d) % chips
        mine = own_rows(core, to)
        there = pl.ds(pl.multiple_of(to * rows, 8), rows)
        gram_part[mine, :] = gram_part[mine, :] + gram_pair[there, :]
        rest_part[core, to] = rest_part[core, to] + rest_pair[to]
        if d > 0:
            sends.append(
                remote(
                    gram_part.at[mine, :],
                    gram_in.at[d - 1],
                    chip_send.at[0, d - 1],
                    chip_recv.at[0, d - 1],
                    chip_at(d),
                )
            )
            sends.append(
                remote(
                    rest_part.at[core, to],
                    rest_in.at[d - 1],
                    chip_send.at[1, d - 1],
                    chip_recv.at[1, d - 1],
                    chip_at(d),
                )
            )
    for copy in sends:
        copy.wait()
    total = gram_part[own_rows(core, chip), :]
    rest = rest_part[core, chip]
    for d in range(chips - 1):
        total = total + gram_in[d]
        rest = rest + rest_in[d]
    piece[...] = total / count
    dose_sums = rest[2 * variants : 3 * variants, :HALF]
    dose_squares = rest[2 * variants : 3 * variants, HALF:]
    means = dose_sums / count
    spread = jnp.sqrt(dose_squares / count - means * means + 1e-05) * math.sqrt(count)
    means = jnp.concatenate([means, means], 1)
    spread = jnp.concatenate([spread, spread], 1)
    for t in range(2):
        at = 3 * variants + 8 * t
        cross = rest[t * variants : (t + 1) * variants]
        own_centred[:, t * WIDE : (t + 1) * WIDE] = (
            cross - means * rest[at : at + 1, :]
        ) / spread

    landing = own_rows(core, chip)
    local = [
        pltpu.make_async_copy(piece, full.at[z, landing, :], local_sem.at[0]),
        pltpu.make_async_copy(own_centred, centred.at[z], local_sem.at[1]),
    ]
    for copy in local:
        copy.start()
    over_z = []
    for d in range(1, groups):
        over_z.append(
            remote(
                piece,
                full.at[z, landing, :],
                z_send.at[0, d - 1],
                z_recv.at[0, d - 1],
                z_at(d),
            )
        )
        over_z.append(
            remote(
                own_centred, centred.at[z], z_send.at[1, d - 1], z_recv.at[1, d - 1], z_at(d)
            )
        )
    plane = [[] for _ in range(groups)]
    to_core = []
    for j in range(groups):
        group = (z - j + groups) % groups
        if j > 0:
            over_z[2 * j - 2].wait_recv()
        held = piece if j == 0 else full.at[group, landing, :]
        for d in range(1, chips):
            plane[j].append(
                remote(
                    held,
                    full.at[group, landing, :],
                    plane_send.at[j, d - 1],
                    plane_recv.at[j, d - 1],
                    chip_at(d),
                )
            )
        to_core.append(
            remote(
                held,
                full.at[group, landing, :],
                core_send.at[j, 0],
                core_recv.at[j, 0],
                partner,
            )
        )
    for j in range(groups):
        group = (z - j + groups) % groups
        for d in range(1, chips):
            plane[j][d - 1].wait_recv()
            came = own_rows(core, (chip - d + chips) % chips)
            to_core.append(
                remote(
                    full.at[group, came, :],
                    full.at[group, came, :],
                    core_send.at[j, d],
                    core_recv.at[j, d],
                    partner,
                )
            )
    for copy in local:
        copy.wait()
    for d in range(1, groups):
        over_z[2 * d - 1].wait_recv()
    for copy in over_z:
        copy.wait_send()
    for j in range(groups):
        for copy in plane[j]:
            copy.wait_send()
    for copy in to_core:
        copy.wait()


def gathered(proteins, dosage):
    groups = lax.axis_size("protein")
    chips = lax.axis_size("sample") // 2
    variants = dosage.shape[1] // (2 * chips)
    gram_rows = (2 * groups + 1) * WIDE
    rows = gram_rows // (2 * chips)
    rest_rows = 3 * variants + 16
    dma = pltpu.SemaphoreType.DMA
    f32 = jnp.float32
    return pl.pallas_call(
        lambda *refs: gather_kernel(chips, groups, *refs),
        out_shape=(
            jax.ShapeDtypeStruct((groups, gram_rows, WIDE), f32),
            jax.ShapeDtypeStruct((groups, variants, 2 * WIDE), f32),
        ),
        in_specs=[pl.BlockSpec(memory_space=pltpu.VMEM)] * 2,
        out_specs=(pl.BlockSpec(memory_space=pl.ANY), pl.BlockSpec(memory_space=pl.ANY)),
        scratch_shapes=[
            pltpu.VMEM((gram_rows, WIDE), f32),
            pltpu.VMEM((2, chips, rest_rows, WIDE), f32),
            pltpu.VMEM((gram_rows // 2, WIDE), f32),
            pltpu.VMEM((chips, rest_rows, WIDE), f32),
            pltpu.VMEM((chips - 1, rows, WIDE), f32),
            pltpu.VMEM((chips - 1, rest_rows, WIDE), f32),
            pltpu.VMEM((rows, WIDE), f32),
            pltpu.VMEM((variants, 2 * WIDE), f32),
            dma((2,)),
            dma((2,)),
            dma((2, chips - 1)),
            dma((2, chips - 1)),
            dma((2, groups - 1)),
            dma((2, groups - 1)),
            dma((groups, chips - 1)),
            dma((groups, chips - 1)),
            dma((groups, chips)),
            dma((groups, chips)),
            dma((2,)),
        ],
        compiler_params=pltpu.CompilerParams(
            collective_id=0, has_side_effects=True, vmem_limit_bytes=48 * 1024 * 1024
        ),
    )(proteins, dosage)


def body(proteins, dosage):
    own = proteins.shape[1] // lax.axis_size("protein") // WIDE
    gram, centred = gathered(proteins, dosage)
    scores = whitened(gram, centred)
    scores = lax.dynamic_slice_in_dim(scores, lax.axis_index("protein") * own, own, 0)
    return jnp.concatenate([scores[p] for p in range(own)], 1)


def solution(mesh):
    in_specs = (P("sample", None), P("sample", None))
    out_specs = P("sample", "protein")
    return jax.shard_map(body, mesh=mesh, in_specs=in_specs, out_specs=out_specs, check_vma=False)
```

```python
import math

import jax
import jax.numpy as jnp
from jax import lax
from jax.experimental import pallas as pl
from jax.experimental.pallas import tpu as pltpu
from jax.sharding import PartitionSpec as P

SUB = 8
HALF = 128
WIDE = 256
CHUNK = 1024


def split(value):
    high = value.astype(jnp.bfloat16)
    low = (value - high.astype(jnp.float32)).astype(jnp.bfloat16)
    return high, low


def dot_nt(left, right):
    return lax.dot_general(
        left, right, (((1,), (1,)), ((), ())), preferred_element_type=jnp.float32
    )


def product_nt(left, right):
    left_high, left_low = left
    right_high, right_low = right
    return dot_nt(
        jnp.concatenate([left_high, left_low, left_high], 1),
        jnp.concatenate([right_high, right_high, right_low], 1),
    )


def exact_dot(left, right):
    return jnp.dot(
        left, right, precision=lax.Precision.HIGHEST, preferred_element_type=jnp.float32
    )


def exact_nt(left, right):
    return lax.dot_general(
        left,
        right,
        (((1,), (1,)), ((), ())),
        precision=lax.Precision.HIGHEST,
        preferred_element_type=jnp.float32,
    )


def inverse_factor(work, inverse):
    for start in range(0, HALF, SUB):
        stop = start + SUB
        rows = work[start:stop, :]
        row = [jnp.broadcast_to(rows[k : k + 1, :], (SUB, 2 * HALF)) for k in range(SUB)]
        col = [
            jnp.broadcast_to(rows[:, start + k : start + k + 1], (SUB, HALF)) for k in range(SUB)
        ]
        entry = [
            [jnp.broadcast_to(col[k][i : i + 1, :], (SUB, HALF)) for k in range(i + 1)]
            for i in range(SUB)
        ]
        scale = [None] * SUB
        lower = [[None] * SUB for _ in range(SUB)]
        for k in range(0, SUB, 2):
            one, cross, two = entry[k][k], entry[k + 1][k], entry[k + 1][k + 1]
            minor = lax.rsqrt(one * two - cross * cross)
            scale[k] = lax.rsqrt(one)
            scale[k + 1] = one * scale[k] * minor
            lower[k + 1][k] = cross * scale[k]
            for i in range(k + 2, SUB):
                lower[i][k] = entry[i][k] * scale[k]
                lower[i][k + 1] = (
                    entry[i][k + 1] - lower[i][k] * lower[k + 1][k]
                ) * scale[k + 1]
            for i in range(k + 2, SUB):
                for m in range(k + 2, i + 1):
                    entry[i][m] = (
                        entry[i][m] - lower[i][k] * lower[m][k] - lower[i][k + 1] * lower[m][k + 1]
                    )
        solved = [None] * SUB
        wide = lambda value: jnp.concatenate([value, value], 1)
        for i in range(SUB):
            total = row[i]
            for k in range(i):
                total = total - wide(lower[i][k]) * solved[k]
            solved[i] = total * wide(scale[i])
        for i in range(SUB):
            inverse[start + i : start + i + 1, :] = solved[i][0:1, HALF:]
        if stop == HALF:
            break
        twice = [None] * SUB
        for i in reversed(range(SUB)):
            total = solved[i]
            for k in range(i + 1, SUB):
                total = total - wide(lower[k][i]) * twice[k]
            twice[i] = total * wide(scale[i])
        for top in range(stop, HALF, SUB):
            block = work[top : top + SUB, :]
            for k in range(SUB):
                factor = jnp.broadcast_to(
                    work[top : top + SUB, start + k : start + k + 1], (SUB, HALF)
                )
                block = block - wide(factor) * twice[k]
            work[top : top + SUB, :] = block


def factor_kernel(gram, centred, out, matrix, work, first, second, full, high, low, sem):
    groups = gram.shape[0]
    panels = 2 * groups
    proteins = panels * WIDE
    variants = centred.shape[1]
    total = proteins + variants
    copies = []
    for z in range(groups):
        cut = (panels - z) * WIDE
        for p, start, size in ((z, 0, cut), (panels - 1 - z, cut, (z + 1) * WIDE)):
            copies.append(
                pltpu.make_async_copy(
                    gram.at[z, pl.ds(start, size), :],
                    matrix.at[p, pl.ds(p * WIDE, size), :],
                    sem.at[p],
                )
            )
    for copy in copies:
        copy.start()
    for z in range(groups):
        matrix[z, proteins:, :] = centred[z, :, :WIDE]
        matrix[panels - 1 - z, proteins:, :] = centred[z, :, WIDE:]
    for copy in copies:
        copy.wait()
    eye = (
        lax.broadcasted_iota(jnp.int32, (HALF, HALF), 0)
        == lax.broadcasted_iota(jnp.int32, (HALF, HALF), 1)
    ).astype(jnp.float32)

    def step(k, carry):
        top = pl.multiple_of(k * WIDE, WIDE)
        mid = pl.multiple_of(k * WIDE + HALF, HALF)
        work[:, :HALF] = matrix[k, pl.ds(top, HALF), :HALF]
        work[:, HALF:] = eye
        inverse_factor(work, first)
        below = exact_nt(matrix[k, pl.ds(mid, HALF), :HALF], first[...])
        work[:, :HALF] = matrix[k, pl.ds(mid, HALF), HALF:] - exact_nt(below, below)
        work[:, HALF:] = eye
        inverse_factor(work, second)
        full[:HALF, :HALF] = first[...]
        full[:HALF, HALF:] = jnp.zeros((HALF, HALF), jnp.float32)
        full[HALF:, :HALF] = -exact_dot(second[...], exact_dot(below, first[...]))
        full[HALF:, HALF:] = second[...]
        inverse = split(full[...])

        def panel_chunk(i, carry):
            base = pl.multiple_of(total - CHUNK * (i + 1), 64)
            block = product_nt(split(matrix[k, pl.ds(base, CHUNK), :]), inverse)
            block_high, block_low = split(block)
            high[pl.ds(base, CHUNK), :] = block_high
            low[pl.ds(base, CHUNK), :] = block_low

            @pl.when(i == 0)
            def _():
                out[k] = block[CHUNK - variants :, :]

            return carry

        rest = total - WIDE * (k + 1)
        lax.fori_loop(0, (rest + CHUNK - 1) // CHUNK, panel_chunk, 0)

        def update(m, carry):
            at = pl.multiple_of(m * WIDE, WIDE)
            right = (high[pl.ds(at, WIDE), :], low[pl.ds(at, WIDE), :])

            def update_chunk(i, carry):
                base = pl.multiple_of(total - CHUNK * (i + 1), 64)
                rows = pl.ds(base, CHUNK)
                matrix[m, rows, :] = matrix[m, rows, :] - product_nt(
                    (high[rows, :], low[rows, :]), right
                )
                return carry

            return lax.fori_loop(0, (total - m * WIDE + CHUNK - 1) // CHUNK, update_chunk, carry)

        lax.fori_loop(k + 1, panels, update, 0)
        return carry

    lax.fori_loop(0, panels, step, 0)


def whitened(gram, centred):
    panels = 2 * gram.shape[0]
    variants = centred.shape[1]
    total = panels * WIDE + variants
    return pl.pallas_call(
        factor_kernel,
        out_shape=jax.ShapeDtypeStruct((panels, variants, WIDE), jnp.float32),
        in_specs=[
            pl.BlockSpec(memory_space=pl.ANY),
            pl.BlockSpec(memory_space=pltpu.VMEM),
        ],
        out_specs=pl.BlockSpec(memory_space=pltpu.VMEM),
        scratch_shapes=[
            pltpu.VMEM((panels, total, WIDE), jnp.float32),
            pltpu.VMEM((HALF, 2 * HALF), jnp.float32),
            pltpu.VMEM((HALF, HALF), jnp.float32),
            pltpu.VMEM((HALF, HALF), jnp.float32),
            pltpu.VMEM((WIDE, WIDE), jnp.float32),
            pltpu.VMEM((total, WIDE), jnp.bfloat16),
            pltpu.VMEM((total, WIDE), jnp.bfloat16),
            pltpu.SemaphoreType.DMA((panels,)),
        ],
        compiler_params=pltpu.CompilerParams(vmem_limit_bytes=48 * 1024 * 1024),
    )(gram, centred)


def dot_tn(left, right):
    return lax.dot_general(
        left, right, (((0,), (0,)), ((), ())), preferred_element_type=jnp.float32
    )


def gather_kernel(
    chips,
    groups,
    proteins,
    dosage,
    full,
    centred,
    gram_part,
    rest_part,
    gram_pair,
    rest_pair,
    gram_in,
    rest_in,
    piece,
    own_centred,
    pair_send,
    pair_recv,
    chip_send,
    chip_recv,
    z_send,
    z_recv,
    plane_send,
    plane_recv,
    core_send,
    core_recv,
    local_sem,
):
    me = lax.axis_index("sample")
    z = lax.axis_index("protein")
    chip, core = me // 2, me % 2
    partner = (chip * 2 + 1 - core, z)
    samples = proteins.shape[0]
    count = samples * 2 * chips
    variants = dosage.shape[1] // (2 * chips)
    rows = full.shape[1] // (2 * chips)
    panels = 2 * groups
    rest_rows = rest_part.shape[2]

    def chip_at(d):
        return (((chip + d) % chips) * 2 + core, z)

    def z_at(d):
        return (me, (z + d) % groups)

    barrier = pltpu.get_barrier_semaphore()
    peers = [partner]
    peers += [chip_at(d) for d in range(1, chips)]
    peers += [z_at(d) for d in range(1, groups)]
    for peer in peers:
        pl.semaphore_signal(barrier, inc=1, device_id=peer, device_id_type=pl.DeviceIdType.MESH)

    def gram_block(i, carry):
        later = (i + z) // panels
        row = pl.multiple_of((z + i - later * (z + 1)) * WIDE, WIDE)
        column = pl.multiple_of((z + later * (panels - 1 - 2 * z)) * WIDE, WIDE)
        gram_part[pl.ds(pl.multiple_of(i * WIDE, WIDE), WIDE), :] = dot_tn(
            proteins[:, pl.ds(row, WIDE)], proteins[:, pl.ds(column, WIDE)]
        )
        return carry

    lax.fori_loop(0, panels + 1, gram_block, 0)
    first = proteins[:, pl.ds(pl.multiple_of(z * WIDE, WIDE), WIDE)]
    last = proteins[:, pl.ds(pl.multiple_of((panels - 1 - z) * WIDE, WIDE), WIDE)]
    ones = jnp.ones((samples, HALF), jnp.bfloat16)
    doses = dosage[...]
    tables = (
        dot_tn(doses, first),
        dot_tn(doses, last),
        jnp.concatenate([dot_tn(doses, ones), dot_tn(doses * doses, ones)], 1),
    )
    sums = [
        jnp.dot(
            jnp.ones((8, samples), jnp.bfloat16), side, preferred_element_type=jnp.float32
        )
        for side in (first, last)
    ]
    for owner in range(2 * chips):
        for t in range(3):
            rest_part[owner % 2, owner // 2, t * variants : (t + 1) * variants, :] = tables[t][
                owner * variants : (owner + 1) * variants
            ]
        for t in range(2):
            at = 3 * variants + 8 * t
            rest_part[owner % 2, owner // 2, at : at + 8, :] = sums[t]
    pl.semaphore_wait(barrier, len(peers))

    def remote(source, target, send, recv, device):
        copy = pltpu.make_async_remote_copy(
            src_ref=source,
            dst_ref=target,
            send_sem=send,
            recv_sem=recv,
            device_id=device,
            device_id_type=pl.DeviceIdType.MESH,
        )
        copy.start()
        return copy

    def own_rows(owner_core, owner_chip):
        return pl.ds(pl.multiple_of((owner_core * chips + owner_chip) * rows, 8), rows)

    half_rows = chips * rows
    pairs = [
        remote(
            gram_part.at[pl.ds(pl.multiple_of((1 - core) * half_rows, 8), half_rows), :],
            gram_pair,
            pair_send.at[0],
            pair_recv.at[0],
            partner,
        ),
        remote(rest_part.at[1 - core], rest_pair, pair_send.at[1], pair_recv.at[1], partner),
    ]
    for copy in pairs:
        copy.wait()
    sends = []
    for d in list(range(1, chips)) + [0]:
        to = (chip + d) % chips
        mine = own_rows(core, to)
        there = pl.ds(pl.multiple_of(to * rows, 8), rows)
        gram_part[mine, :] = gram_part[mine, :] + gram_pair[there, :]
        rest_part[core, to] = rest_part[core, to] + rest_pair[to]
        if d > 0:
            sends.append(
                remote(
                    gram_part.at[mine, :],
                    gram_in.at[d - 1],
                    chip_send.at[0, d - 1],
                    chip_recv.at[0, d - 1],
                    chip_at(d),
                )
            )
            sends.append(
                remote(
                    rest_part.at[core, to],
                    rest_in.at[d - 1],
                    chip_send.at[1, d - 1],
                    chip_recv.at[1, d - 1],
                    chip_at(d),
                )
            )
    for copy in sends:
        copy.wait()
    total = gram_part[own_rows(core, chip), :]
    rest = rest_part[core, chip]
    for d in range(chips - 1):
        total = total + gram_in[d]
        rest = rest + rest_in[d]
    piece[...] = total / count
    dose_sums = rest[2 * variants : 3 * variants, :HALF]
    dose_squares = rest[2 * variants : 3 * variants, HALF:]
    means = dose_sums / count
    spread = jnp.sqrt(dose_squares / count - means * means + 1e-05) * math.sqrt(count)
    means = jnp.concatenate([means, means], 1)
    spread = jnp.concatenate([spread, spread], 1)
    for t in range(2):
        at = 3 * variants + 8 * t
        cross = rest[t * variants : (t + 1) * variants]
        own_centred[:, t * WIDE : (t + 1) * WIDE] = (
            cross - means * rest[at : at + 1, :]
        ) / spread

    near = 2 if chips == 4 else chips - 1

    def chip_near(d):
        if near == chips - 1:
            return (chip + d) % chips
        return chip + 1 - 2 * (chip % 2) if d == 1 else (chip + 2) % 4

    def chip_from(d):
        if near == chips - 1:
            return (chip - d + chips) % chips
        return chip_near(d)

    landing = own_rows(core, chip)
    local = [
        pltpu.make_async_copy(piece, full.at[z, landing, :], local_sem.at[0]),
        pltpu.make_async_copy(own_centred, centred.at[z], local_sem.at[1]),
    ]
    for copy in local:
        copy.start()
    over_z = []
    for d in range(1, groups):
        over_z.append(
            remote(
                piece,
                full.at[z, landing, :],
                z_send.at[0, d - 1],
                z_recv.at[0, d - 1],
                z_at(d),
            )
        )
        over_z.append(
            remote(
                own_centred, centred.at[z], z_send.at[1, d - 1], z_recv.at[1, d - 1], z_at(d)
            )
        )
    plane = [[] for _ in range(groups)]
    to_core = []
    for j in range(groups):
        group = (z - j + groups) % groups
        if j > 0:
            over_z[2 * j - 2].wait_recv()
        held = piece if j == 0 else full.at[group, landing, :]
        for d in range(1, near + 1):
            plane[j].append(
                remote(
                    held,
                    full.at[group, landing, :],
                    plane_send.at[j, d - 1],
                    plane_recv.at[j, d - 1],
                    (chip_near(d) * 2 + core, z),
                )
            )
        to_core.append(
            remote(
                held,
                full.at[group, landing, :],
                core_send.at[j, 0],
                core_recv.at[j, 0],
                partner,
            )
        )
    for j in range(groups):
        group = (z - j + groups) % groups
        for d in range(1, near + 1):
            plane[j][d - 1].wait_recv()
            came = own_rows(core, chip_from(d))
            if near < chips - 1 and d == 2 - j % 2:
                plane[j].append(
                    remote(
                        full.at[group, came, :],
                        full.at[group, came, :],
                        plane_send.at[j, near],
                        plane_recv.at[j, near],
                        (chip_near(3 - d) * 2 + core, z),
                    )
                )
            to_core.append(
                remote(
                    full.at[group, came, :],
                    full.at[group, came, :],
                    core_send.at[j, d],
                    core_recv.at[j, d],
                    partner,
                )
            )
    if near < chips - 1:
        for j in range(groups):
            group = (z - j + groups) % groups
            plane[j][near].wait_recv()
            came = own_rows(core, 3 - chip)
            to_core.append(
                remote(
                    full.at[group, came, :],
                    full.at[group, came, :],
                    core_send.at[j, chips - 1],
                    core_recv.at[j, chips - 1],
                    partner,
                )
            )
    for copy in local:
        copy.wait()
    for d in range(1, groups):
        over_z[2 * d - 1].wait_recv()
    for copy in over_z:
        copy.wait_send()
    for j in range(groups):
        for copy in plane[j]:
            copy.wait_send()
    for copy in to_core:
        copy.wait()


def gathered(proteins, dosage):
    groups = lax.axis_size("protein")
    chips = lax.axis_size("sample") // 2
    variants = dosage.shape[1] // (2 * chips)
    gram_rows = (2 * groups + 1) * WIDE
    rows = gram_rows // (2 * chips)
    rest_rows = 3 * variants + 16
    dma = pltpu.SemaphoreType.DMA
    f32 = jnp.float32
    return pl.pallas_call(
        lambda *refs: gather_kernel(chips, groups, *refs),
        out_shape=(
            jax.ShapeDtypeStruct((groups, gram_rows, WIDE), f32),
            jax.ShapeDtypeStruct((groups, variants, 2 * WIDE), f32),
        ),
        in_specs=[pl.BlockSpec(memory_space=pltpu.VMEM)] * 2,
        out_specs=(pl.BlockSpec(memory_space=pl.ANY), pl.BlockSpec(memory_space=pl.ANY)),
        scratch_shapes=[
            pltpu.VMEM((gram_rows, WIDE), f32),
            pltpu.VMEM((2, chips, rest_rows, WIDE), f32),
            pltpu.VMEM((gram_rows // 2, WIDE), f32),
            pltpu.VMEM((chips, rest_rows, WIDE), f32),
            pltpu.VMEM((chips - 1, rows, WIDE), f32),
            pltpu.VMEM((chips - 1, rest_rows, WIDE), f32),
            pltpu.VMEM((rows, WIDE), f32),
            pltpu.VMEM((variants, 2 * WIDE), f32),
            dma((2,)),
            dma((2,)),
            dma((2, chips - 1)),
            dma((2, chips - 1)),
            dma((2, groups - 1)),
            dma((2, groups - 1)),
            dma((groups, chips - 1)),
            dma((groups, chips - 1)),
            dma((groups, chips)),
            dma((groups, chips)),
            dma((2,)),
        ],
        compiler_params=pltpu.CompilerParams(
            collective_id=0, has_side_effects=True, vmem_limit_bytes=48 * 1024 * 1024
        ),
    )(proteins, dosage)


def body(proteins, dosage):
    own = proteins.shape[1] // lax.axis_size("protein") // WIDE
    gram, centred = gathered(proteins, dosage)
    scores = whitened(gram, centred)
    scores = lax.dynamic_slice_in_dim(scores, lax.axis_index("protein") * own, own, 0)
    return jnp.concatenate([scores[p] for p in range(own)], 1)


def solution(mesh):
    in_specs = (P("sample", None), P("sample", None))
    out_specs = P("sample", "protein")
    return jax.shard_map(body, mesh=mesh, in_specs=in_specs, out_specs=out_specs, check_vma=False)
```

```python
import math

import jax
import jax.numpy as jnp
from jax import lax
from jax.experimental import pallas as pl
from jax.experimental.pallas import tpu as pltpu
from jax.sharding import PartitionSpec as P

SUB = 8
HALF = 128
WIDE = 256
CHUNK = 1024


def split(value):
    high = value.astype(jnp.bfloat16)
    low = (value - high.astype(jnp.float32)).astype(jnp.bfloat16)
    return high, low


def dot_nt(left, right):
    return lax.dot_general(
        left, right, (((1,), (1,)), ((), ())), preferred_element_type=jnp.float32
    )


def product_nt(left, right):
    left_high, left_low = left
    right_high, right_low = right
    return dot_nt(
        jnp.concatenate([left_high, left_low, left_high], 1),
        jnp.concatenate([right_high, right_high, right_low], 1),
    )


def exact_dot(left, right):
    return jnp.dot(
        left, right, precision=lax.Precision.HIGHEST, preferred_element_type=jnp.float32
    )


def inverse_factor(work, inverse):
    for start in range(0, HALF, SUB):
        stop = start + SUB
        rows = work[start:stop, :]
        row = [jnp.broadcast_to(rows[k : k + 1, :], (SUB, 2 * HALF)) for k in range(SUB)]
        col = [
            jnp.broadcast_to(rows[:, start + k : start + k + 1], (SUB, HALF)) for k in range(SUB)
        ]
        entry = [
            [jnp.broadcast_to(col[k][i : i + 1, :], (SUB, HALF)) for k in range(i + 1)]
            for i in range(SUB)
        ]
        scale = [None] * SUB
        lower = [[None] * SUB for _ in range(SUB)]
        for k in range(0, SUB, 2):
            one, cross, two = entry[k][k], entry[k + 1][k], entry[k + 1][k + 1]
            minor = lax.rsqrt(one * two - cross * cross)
            scale[k] = lax.rsqrt(one)
            scale[k + 1] = one * scale[k] * minor
            lower[k + 1][k] = cross * scale[k]
            for i in range(k + 2, SUB):
                lower[i][k] = entry[i][k] * scale[k]
                lower[i][k + 1] = (
                    entry[i][k + 1] - lower[i][k] * lower[k + 1][k]
                ) * scale[k + 1]
            for i in range(k + 2, SUB):
                for m in range(k + 2, i + 1):
                    entry[i][m] = (
                        entry[i][m] - lower[i][k] * lower[m][k] - lower[i][k + 1] * lower[m][k + 1]
                    )
        solved = [None] * SUB
        wide = lambda value: jnp.concatenate([value, value], 1)
        for i in range(SUB):
            total = row[i]
            for k in range(i):
                total = total - wide(lower[i][k]) * solved[k]
            solved[i] = total * wide(scale[i])
        for i in range(SUB):
            inverse[start + i : start + i + 1, :] = solved[i][0:1, HALF:]
        if stop == HALF:
            break
        twice = [None] * SUB
        for i in reversed(range(SUB)):
            total = solved[i]
            for k in range(i + 1, SUB):
                total = total - wide(lower[k][i]) * twice[k]
            twice[i] = total * wide(scale[i])
        for top in range(stop, HALF, SUB):
            block = work[top : top + SUB, :]
            for k in range(SUB):
                factor = jnp.broadcast_to(
                    work[top : top + SUB, start + k : start + k + 1], (SUB, HALF)
                )
                block = block - wide(factor) * twice[k]
            work[top : top + SUB, :] = block


def factor_kernel(gram, centred, out, matrix, work, first, second, full, high, low, sem):
    groups = gram.shape[0]
    panels = 2 * groups
    proteins = panels * WIDE
    variants = centred.shape[1]
    total = proteins + variants
    copies = []
    for z in range(groups):
        cut = (panels - z) * WIDE
        for p, start, size in ((z, 0, cut), (panels - 1 - z, cut, (z + 1) * WIDE)):
            copies.append(
                pltpu.make_async_copy(
                    gram.at[z, pl.ds(start, size), :],
                    matrix.at[p, pl.ds(p * WIDE, size), :],
                    sem.at[p],
                )
            )
    for copy in copies:
        copy.start()
    for z in range(groups):
        matrix[z, proteins:, :] = centred[z, :, :WIDE]
        matrix[panels - 1 - z, proteins:, :] = centred[z, :, WIDE:]
    for copy in copies:
        copy.wait()
    eye = (
        lax.broadcasted_iota(jnp.int32, (HALF, HALF), 0)
        == lax.broadcasted_iota(jnp.int32, (HALF, HALF), 1)
    ).astype(jnp.float32)

    def step(k, carry):
        top = pl.multiple_of(k * WIDE, WIDE)
        mid = pl.multiple_of(k * WIDE + HALF, HALF)
        work[:, :HALF] = matrix[k, pl.ds(top, HALF), :HALF]
        work[:, HALF:] = eye
        inverse_factor(work, first)
        below = product_nt(split(matrix[k, pl.ds(mid, HALF), :HALF]), split(first[...]))
        work[:, :HALF] = matrix[k, pl.ds(mid, HALF), HALF:] - product_nt(split(below), split(below))
        work[:, HALF:] = eye
        inverse_factor(work, second)
        full[:HALF, :HALF] = first[...]
        full[:HALF, HALF:] = jnp.zeros((HALF, HALF), jnp.float32)
        full[HALF:, :HALF] = -exact_dot(second[...], exact_dot(below, first[...]))
        full[HALF:, HALF:] = second[...]
        inverse = split(full[...])

        def panel_chunk(i, carry):
            base = pl.multiple_of(total - CHUNK * (i + 1), 64)
            block = product_nt(split(matrix[k, pl.ds(base, CHUNK), :]), inverse)
            block_high, block_low = split(block)
            high[pl.ds(base, CHUNK), :] = block_high
            low[pl.ds(base, CHUNK), :] = block_low

            @pl.when(i == 0)
            def _():
                out[k] = block[CHUNK - variants :, :]

            return carry

        rest = total - WIDE * (k + 1)
        lax.fori_loop(0, (rest + CHUNK - 1) // CHUNK, panel_chunk, 0)

        def update(m, carry):
            at = pl.multiple_of(m * WIDE, WIDE)
            right = (high[pl.ds(at, WIDE), :], low[pl.ds(at, WIDE), :])

            def update_chunk(i, carry):
                base = pl.multiple_of(total - CHUNK * (i + 1), 64)
                rows = pl.ds(base, CHUNK)
                matrix[m, rows, :] = matrix[m, rows, :] - product_nt(
                    (high[rows, :], low[rows, :]), right
                )
                return carry

            return lax.fori_loop(0, (total - m * WIDE + CHUNK - 1) // CHUNK, update_chunk, carry)

        lax.fori_loop(k + 1, panels, update, 0)
        return carry

    lax.fori_loop(0, panels, step, 0)


def whitened(gram, centred):
    panels = 2 * gram.shape[0]
    variants = centred.shape[1]
    total = panels * WIDE + variants
    return pl.pallas_call(
        factor_kernel,
        out_shape=jax.ShapeDtypeStruct((panels, variants, WIDE), jnp.float32),
        in_specs=[
            pl.BlockSpec(memory_space=pl.ANY),
            pl.BlockSpec(memory_space=pltpu.VMEM),
        ],
        out_specs=pl.BlockSpec(memory_space=pltpu.VMEM),
        scratch_shapes=[
            pltpu.VMEM((panels, total, WIDE), jnp.float32),
            pltpu.VMEM((HALF, 2 * HALF), jnp.float32),
            pltpu.VMEM((HALF, HALF), jnp.float32),
            pltpu.VMEM((HALF, HALF), jnp.float32),
            pltpu.VMEM((WIDE, WIDE), jnp.float32),
            pltpu.VMEM((total, WIDE), jnp.bfloat16),
            pltpu.VMEM((total, WIDE), jnp.bfloat16),
            pltpu.SemaphoreType.DMA((panels,)),
        ],
        compiler_params=pltpu.CompilerParams(vmem_limit_bytes=48 * 1024 * 1024),
    )(gram, centred)


def dot_tn(left, right):
    return lax.dot_general(
        left, right, (((0,), (0,)), ((), ())), preferred_element_type=jnp.float32
    )


def gather_kernel(
    chips,
    groups,
    proteins,
    dosage,
    full,
    centred,
    gram_part,
    rest_part,
    gram_pair,
    rest_pair,
    gram_in,
    rest_in,
    piece,
    own_centred,
    pair_send,
    pair_recv,
    chip_send,
    chip_recv,
    z_send,
    z_recv,
    plane_send,
    plane_recv,
    core_send,
    core_recv,
    local_sem,
):
    me = lax.axis_index("sample")
    z = lax.axis_index("protein")
    chip, core = me // 2, me % 2
    partner = (chip * 2 + 1 - core, z)
    samples = proteins.shape[0]
    count = samples * 2 * chips
    variants = dosage.shape[1] // (2 * chips)
    rows = full.shape[1] // (2 * chips)
    panels = 2 * groups
    rest_rows = rest_part.shape[2]

    def chip_at(d):
        return (((chip + d) % chips) * 2 + core, z)

    def z_at(d):
        return (me, (z + d) % groups)

    barrier = pltpu.get_barrier_semaphore()
    peers = [partner]
    peers += [chip_at(d) for d in range(1, chips)]
    peers += [z_at(d) for d in range(1, groups)]
    for peer in peers:
        pl.semaphore_signal(barrier, inc=1, device_id=peer, device_id_type=pl.DeviceIdType.MESH)

    def gram_block(i, carry):
        later = (i + z) // panels
        row = pl.multiple_of((z + i - later * (z + 1)) * WIDE, WIDE)
        column = pl.multiple_of((z + later * (panels - 1 - 2 * z)) * WIDE, WIDE)
        gram_part[pl.ds(pl.multiple_of(i * WIDE, WIDE), WIDE), :] = dot_tn(
            proteins[:, pl.ds(row, WIDE)], proteins[:, pl.ds(column, WIDE)]
        )
        return carry

    lax.fori_loop(0, panels + 1, gram_block, 0)
    first = proteins[:, pl.ds(pl.multiple_of(z * WIDE, WIDE), WIDE)]
    last = proteins[:, pl.ds(pl.multiple_of((panels - 1 - z) * WIDE, WIDE), WIDE)]
    ones = jnp.ones((samples, HALF), jnp.bfloat16)
    doses = dosage[...]
    tables = (
        dot_tn(doses, first),
        dot_tn(doses, last),
        jnp.concatenate([dot_tn(doses, ones), dot_tn(doses * doses, ones)], 1),
    )
    sums = [
        jnp.dot(
            jnp.ones((8, samples), jnp.bfloat16), side, preferred_element_type=jnp.float32
        )
        for side in (first, last)
    ]
    for owner in range(2 * chips):
        for t in range(3):
            rest_part[owner % 2, owner // 2, t * variants : (t + 1) * variants, :] = tables[t][
                owner * variants : (owner + 1) * variants
            ]
        for t in range(2):
            at = 3 * variants + 8 * t
            rest_part[owner % 2, owner // 2, at : at + 8, :] = sums[t]
    pl.semaphore_wait(barrier, len(peers))

    def remote(source, target, send, recv, device):
        copy = pltpu.make_async_remote_copy(
            src_ref=source,
            dst_ref=target,
            send_sem=send,
            recv_sem=recv,
            device_id=device,
            device_id_type=pl.DeviceIdType.MESH,
        )
        copy.start()
        return copy

    def own_rows(owner_core, owner_chip):
        return pl.ds(pl.multiple_of((owner_core * chips + owner_chip) * rows, 8), rows)

    half_rows = chips * rows
    pairs = [
        remote(
            gram_part.at[pl.ds(pl.multiple_of((1 - core) * half_rows, 8), half_rows), :],
            gram_pair,
            pair_send.at[0],
            pair_recv.at[0],
            partner,
        ),
        remote(rest_part.at[1 - core], rest_pair, pair_send.at[1], pair_recv.at[1], partner),
    ]
    for copy in pairs:
        copy.wait()
    sends = []
    for d in list(range(1, chips)) + [0]:
        to = (chip + d) % chips
        mine = own_rows(core, to)
        there = pl.ds(pl.multiple_of(to * rows, 8), rows)
        gram_part[mine, :] = gram_part[mine, :] + gram_pair[there, :]
        rest_part[core, to] = rest_part[core, to] + rest_pair[to]
        if d > 0:
            sends.append(
                remote(
                    gram_part.at[mine, :],
                    gram_in.at[d - 1],
                    chip_send.at[0, d - 1],
                    chip_recv.at[0, d - 1],
                    chip_at(d),
                )
            )
            sends.append(
                remote(
                    rest_part.at[core, to],
                    rest_in.at[d - 1],
                    chip_send.at[1, d - 1],
                    chip_recv.at[1, d - 1],
                    chip_at(d),
                )
            )
    for copy in sends:
        copy.wait()
    total = gram_part[own_rows(core, chip), :]
    rest = rest_part[core, chip]
    for d in range(chips - 1):
        total = total + gram_in[d]
        rest = rest + rest_in[d]
    piece[...] = total / count
    dose_sums = rest[2 * variants : 3 * variants, :HALF]
    dose_squares = rest[2 * variants : 3 * variants, HALF:]
    means = dose_sums / count
    spread = jnp.sqrt(dose_squares / count - means * means + 1e-05) * math.sqrt(count)
    means = jnp.concatenate([means, means], 1)
    spread = jnp.concatenate([spread, spread], 1)
    for t in range(2):
        at = 3 * variants + 8 * t
        cross = rest[t * variants : (t + 1) * variants]
        own_centred[:, t * WIDE : (t + 1) * WIDE] = (
            cross - means * rest[at : at + 1, :]
        ) / spread

    near = 2 if chips == 4 else chips - 1

    def chip_near(d):
        if near == chips - 1:
            return (chip + d) % chips
        return chip + 1 - 2 * (chip % 2) if d == 1 else (chip + 2) % 4

    def chip_from(d):
        if near == chips - 1:
            return (chip - d + chips) % chips
        return chip_near(d)

    landing = own_rows(core, chip)
    local = [
        pltpu.make_async_copy(piece, full.at[z, landing, :], local_sem.at[0]),
        pltpu.make_async_copy(own_centred, centred.at[z], local_sem.at[1]),
    ]
    for copy in local:
        copy.start()
    over_z = []
    for d in range(1, groups):
        over_z.append(
            remote(
                piece,
                full.at[z, landing, :],
                z_send.at[0, d - 1],
                z_recv.at[0, d - 1],
                z_at(d),
            )
        )
        over_z.append(
            remote(
                own_centred, centred.at[z], z_send.at[1, d - 1], z_recv.at[1, d - 1], z_at(d)
            )
        )
    plane = [[] for _ in range(groups)]
    to_core = []
    for j in range(groups):
        group = (z - j + groups) % groups
        if j > 0:
            over_z[2 * j - 2].wait_recv()
        held = piece if j == 0 else full.at[group, landing, :]
        for d in range(1, near + 1):
            plane[j].append(
                remote(
                    held,
                    full.at[group, landing, :],
                    plane_send.at[j, d - 1],
                    plane_recv.at[j, d - 1],
                    (chip_near(d) * 2 + core, z),
                )
            )
        to_core.append(
            remote(
                held,
                full.at[group, landing, :],
                core_send.at[j, 0],
                core_recv.at[j, 0],
                partner,
            )
        )
    for j in range(groups):
        group = (z - j + groups) % groups
        for d in range(1, near + 1):
            plane[j][d - 1].wait_recv()
            came = own_rows(core, chip_from(d))
            if near < chips - 1 and d == 2 - j % 2:
                plane[j].append(
                    remote(
                        full.at[group, came, :],
                        full.at[group, came, :],
                        plane_send.at[j, near],
                        plane_recv.at[j, near],
                        (chip_near(3 - d) * 2 + core, z),
                    )
                )
            to_core.append(
                remote(
                    full.at[group, came, :],
                    full.at[group, came, :],
                    core_send.at[j, d],
                    core_recv.at[j, d],
                    partner,
                )
            )
    if near < chips - 1:
        for j in range(groups):
            group = (z - j + groups) % groups
            plane[j][near].wait_recv()
            came = own_rows(core, 3 - chip)
            to_core.append(
                remote(
                    full.at[group, came, :],
                    full.at[group, came, :],
                    core_send.at[j, chips - 1],
                    core_recv.at[j, chips - 1],
                    partner,
                )
            )
    for copy in local:
        copy.wait()
    for d in range(1, groups):
        over_z[2 * d - 1].wait_recv()
    for copy in over_z:
        copy.wait_send()
    for j in range(groups):
        for copy in plane[j]:
            copy.wait_send()
    for copy in to_core:
        copy.wait()


def gathered(proteins, dosage):
    groups = lax.axis_size("protein")
    chips = lax.axis_size("sample") // 2
    variants = dosage.shape[1] // (2 * chips)
    gram_rows = (2 * groups + 1) * WIDE
    rows = gram_rows // (2 * chips)
    rest_rows = 3 * variants + 16
    dma = pltpu.SemaphoreType.DMA
    f32 = jnp.float32
    return pl.pallas_call(
        lambda *refs: gather_kernel(chips, groups, *refs),
        out_shape=(
            jax.ShapeDtypeStruct((groups, gram_rows, WIDE), f32),
            jax.ShapeDtypeStruct((groups, variants, 2 * WIDE), f32),
        ),
        in_specs=[pl.BlockSpec(memory_space=pltpu.VMEM)] * 2,
        out_specs=(pl.BlockSpec(memory_space=pl.ANY), pl.BlockSpec(memory_space=pl.ANY)),
        scratch_shapes=[
            pltpu.VMEM((gram_rows, WIDE), f32),
            pltpu.VMEM((2, chips, rest_rows, WIDE), f32),
            pltpu.VMEM((gram_rows // 2, WIDE), f32),
            pltpu.VMEM((chips, rest_rows, WIDE), f32),
            pltpu.VMEM((chips - 1, rows, WIDE), f32),
            pltpu.VMEM((chips - 1, rest_rows, WIDE), f32),
            pltpu.VMEM((rows, WIDE), f32),
            pltpu.VMEM((variants, 2 * WIDE), f32),
            dma((2,)),
            dma((2,)),
            dma((2, chips - 1)),
            dma((2, chips - 1)),
            dma((2, groups - 1)),
            dma((2, groups - 1)),
            dma((groups, chips - 1)),
            dma((groups, chips - 1)),
            dma((groups, chips)),
            dma((groups, chips)),
            dma((2,)),
        ],
        compiler_params=pltpu.CompilerParams(
            collective_id=0, has_side_effects=True, vmem_limit_bytes=48 * 1024 * 1024
        ),
    )(proteins, dosage)


def body(proteins, dosage):
    own = proteins.shape[1] // lax.axis_size("protein") // WIDE
    gram, centred = gathered(proteins, dosage)
    scores = whitened(gram, centred)
    scores = lax.dynamic_slice_in_dim(scores, lax.axis_index("protein") * own, own, 0)
    return jnp.concatenate([scores[p] for p in range(own)], 1)


def solution(mesh):
    in_specs = (P("sample", None), P("sample", None))
    out_specs = P("sample", "protein")
    return jax.shard_map(body, mesh=mesh, in_specs=in_specs, out_specs=out_specs, check_vma=False)
```
